32 devices in a mesh: groups: 2 (over x), beam: 8 (over z, y), sub: 2 (over core).
Axes of the slice: x: 2, y: 2, z: 4, core: 2. Of those that a mesh axis runs over, the one named last changes fastest.
Arguments:
- intensities: bfloat16 [32, 16384, 270], P('groups', ('beam', 'sub')), parts along dimension 0, may hold values from -0.046875 to 0.046875
- sweep_delays: int32 [16384, 16], replicated, may hold values from 0 to 7
- band_offsets: int32 [16, 1024], replicated, may hold values from 0 to 7
- coarse_trial: int32 [1024], replicated, may hold values from 0 to 15
Outputs:
- dm_planes: float32 [1024, 32, 256], P('sub', ('groups', 'beam')), parts along dimension 1
The draws below stay inside these ranges and needn't reach their ends.
There are 2 independent parts, one for each index of `groups`. The reference program is written for one: setup_inputs(seed, part) draws one part's arguments, and reference() takes and returns one part's arrays. A program takes and returns all parts, laid end to end along the dimension named above; an argument that names none is the same for every part. Nothing has to cross between parts.
All inputs are finite; a program needn't handle non-finite values.
Results may differ from the reference program's by a relative error of at most 0.0029.
Values may be sent and summed in bfloat16 or wider, within the bound.
A program may use at most 128 MiB of HBM per device.

```python
import jax
import jax.numpy as jnp
from jax import lax

CHANNELS = 16384
TRIALS = 1024
SUBBANDS = 16
COARSE = 16
BAND_LAGS = 8
SUB_LAGS = 8
SAMPLES = 256
BEAMS = 16
SHARD = 1024
HALVES = 2
OUT_LEN = 263
SPAN = 270


def set_ends(entries, own_key, least, top_value):
    shape = entries.shape
    index_at = [jax.random.randint(jax.random.fold_in(own_key, axis), (), 0, shape[axis]) for axis in range(len(shape))]
    entries = entries.at[tuple(index_at)].set(least)
    longest = shape.index(max(shape))
    index_at[longest] = (index_at[longest] + 1) % shape[longest]
    return entries.at[tuple(index_at)].set(top_value)


def steps_of(stream_key, dims, pieces, low, top_value):
    def one(position, blocks):
        draws = jax.random.uniform(jax.random.fold_in(jax.random.fold_in(stream_key, 6), position), (blocks,), jnp.float32, low / len(pieces), top_value / len(pieces))
        return jnp.repeat(jnp.exp(draws), dims[position] // blocks).reshape((-1,) + (1,) * (len(dims) - position - 1))

    gain = one(*pieces[0])
    for cut in pieces[1:]:
        gain = gain * one(*cut)
    return gain


def bell_draw(own_key, dims, scale, reach, split=(), kind=jnp.bfloat16):
    entries = scale * jax.random.normal(own_key, dims, jnp.float32)
    if split:
        entries = entries * steps_of(own_key, dims, split, -0.22, 0.18)
    return jnp.clip(entries, -reach, reach).astype(kind)


def setup_inputs(seed: int = 0, part: int = 0) -> dict:
    streams_of = jax.random.split(jax.random.key(seed), 5)
    own_keys = jax.random.split(jax.random.fold_in(streams_of[4], part), 5)
    intensities = bell_draw(own_keys[0], (BEAMS, CHANNELS, SPAN), (CHANNELS ** -0.5), 0.046875, ((1, 16),))
    sweep_delays = set_ends(jax.random.randint(streams_of[1], (CHANNELS, COARSE), 0, BAND_LAGS), jax.random.fold_in(streams_of[1], 1), 0, BAND_LAGS - 1).astype(jnp.int32)
    band_offsets = set_ends(jax.random.randint(streams_of[2], (SUBBANDS, TRIALS), 0, SUB_LAGS), jax.random.fold_in(streams_of[2], 1), 0, SUB_LAGS - 1).astype(jnp.int32)
    coarse_trial = set_ends(jax.random.randint(streams_of[3], (TRIALS,), 0, COARSE), jax.random.fold_in(streams_of[3], 1), 0, COARSE - 1).astype(jnp.int32)
    return {"intensities": intensities, "sweep_delays": sweep_delays, "band_offsets": band_offsets, "coarse_trial": coarse_trial}


def reference(intensities, sweep_delays, band_offsets, coarse_trial):
    times = jnp.arange(OUT_LEN, dtype=jnp.int32)
    rows = jnp.arange(CHANNELS, dtype=jnp.int32)[None, :, None]
    index = sweep_delays.T.astype(jnp.int32)[:, :, None] + times[None, None, :]
    out_times = jnp.arange(SAMPLES, dtype=jnp.int32)
    shift_index = band_offsets.astype(jnp.int32)[:, :, None] + out_times[None, None, :]
    subs = jnp.arange(SUBBANDS, dtype=jnp.int32)[:, None, None]
    trial_index = coarse_trial.astype(jnp.int32)[None, :, None]
    channel_ids = jnp.arange(CHANNELS, dtype=jnp.int32)
    classes = ((channel_ids // SHARD) % HALVES) * SUBBANDS + channel_ids // (CHANNELS // SUBBANDS)
    members = (classes[:, None] == jnp.arange(HALVES * SUBBANDS, dtype=jnp.int32)[None, :]).astype(jnp.float32)

    def one_beam(block):
        picked = block[rows, index].astype(jnp.float32)
        summed = jnp.einsum("cfo,fk->kco", picked, members, precision=lax.Precision.HIGHEST)
        rounded = lax.optimization_barrier(summed.astype(jnp.bfloat16)).astype(jnp.float32)
        rounded = rounded.reshape(HALVES, SUBBANDS, COARSE, OUT_LEN)
        chosen = rounded[:, subs, trial_index, shift_index]
        return jnp.sum(chosen, axis=(0, 1))

    planes = lax.map(one_beam, intensities)
    return jnp.transpose(planes, (1, 0, 2))
```

```python
import jax
import jax.numpy as jnp
from jax import lax
from jax.experimental import pallas as pl
from jax.experimental.pallas import tpu as pltpu
from jax.sharding import PartitionSpec as P

CHANNELS = 16384
SUBBANDS = 16
COARSE = 16
BAND_LAGS = 8
SUB_LAGS = 8


def section_one(intens, delays, bands, span_out, groups):
    count_beams, chans, span = intens.shape
    block = min(chans, 1024)
    cols = groups * COARSE
    members = jnp.arange(groups, dtype=jnp.int32)
    lag_ids = jnp.arange(BAND_LAGS, dtype=jnp.int32)

    def add_block(index, total):
        member = bands[:, None] == members[None, :]
        lag_hit = delays[:, None, :] == lag_ids[None, :, None]
        table = (
            (member[:, None, :, None] & lag_hit[:, :, None, :])
            .reshape(block, BAND_LAGS * cols)
            .astype(jnp.bfloat16)
        )
        return total + jnp.einsum("bct,cn->btn", intens, table, preferred_element_type=jnp.float32)

    empty = jnp.zeros((count_beams, span, BAND_LAGS * cols), jnp.float32)
    spread = lax.fori_loop(0, chans // block, add_block, empty)
    result = spread[:, 0:span_out, 0:cols]
    for lag in range(1, BAND_LAGS):
        result = result + spread[:, lag : lag + span_out, lag * cols : (lag + 1) * cols]
    return result


def section_two(planes, offsets, coarse_map, count):
    halves_here, beams_here, span_out, cols = planes.shape
    samples = span_out - SUB_LAGS + 1
    coarse_hit = coarse_map[None, :] == jnp.arange(COARSE, dtype=jnp.int32)[:, None]
    total = jnp.zeros((count, beams_here, samples), jnp.float32)
    for lag in range(SUB_LAGS):
        table = (
            ((offsets == lag)[:, None, :] & coarse_hit[None, :, :])
            .reshape(cols, count)
            .astype(jnp.bfloat16)
        )
        total = total + jnp.einsum(
            "hbtn,nm->mbt",
            planes[:, :, lag : lag + samples, :],
            table,
            preferred_element_type=jnp.float32,
        )
    return total


def on_device(intensities, sweep_delays, band_offsets, coarse_trial):
    beams_all, chans_local, span = intensities.shape
    beam_count = lax.axis_size("beam")
    sub_count = lax.axis_size("sub")
    per_device = beams_all // beam_count
    out_len = span - BAND_LAGS + 1
    trials_local = band_offsets.shape[1] // sub_count
    sub_width = CHANNELS // SUBBANDS
    sub_here = lax.axis_index("sub")
    held = max(1, chans_local // sub_width)
    first = (lax.axis_index("beam") * sub_count + sub_here) * chans_local
    delay_view = lax.dynamic_slice_in_dim(sweep_delays, first, chans_local, 0)
    band_view = (first + jnp.arange(chans_local, dtype=jnp.int32)) // sub_width - first // sub_width
    local_terms = section_one(intensities, delay_view, band_view, out_len, held)
    grouped = local_terms.reshape(beam_count, per_device, out_len, held * COARSE)
    arrived = lax.all_to_all(grouped, "beam", split_axis=0, concat_axis=0, tiled=True)
    arrived = arrived.reshape(beam_count, per_device, out_len, held, COARSE)
    source_first = (
        (jnp.arange(beam_count, dtype=jnp.int32) * sub_count + sub_here) * chans_local // sub_width
    )
    target = source_first[:, None] + jnp.arange(held, dtype=jnp.int32)[None, :]
    placing = (target[:, :, None] == jnp.arange(SUBBANDS, dtype=jnp.int32)[None, None, :]).astype(
        jnp.float32
    )
    planes = jnp.einsum(
        "ibtpc,ips->btsc", arrived, placing, precision=lax.Precision.HIGHEST
    ).reshape(per_device, out_len, SUBBANDS * COARSE)
    rounded = planes.astype(jnp.bfloat16)
    return lax.psum_scatter(
        section_two(rounded[None], band_offsets, coarse_trial, lax.axis_size("sub") * trials_local),
        "sub",
        scatter_dimension=0,
        tiled=True,
    )


SAMPLE_LANES = 128
CHUNK_TIMES = 30


def planes_kernel(
    x_hbm,
    delays_hbm,
    offsets_hbm,
    coarse_hbm,
    planes_out,
    key_out,
    x_vmem,
    delays_vmem,
    offsets_vmem,
    coarse_vmem,
    table,
    spread,
    send,
    recv,
    x_sem,
    small_sem,
    send_sem,
    recv_sem,
    pass_send_sem,
    pass_recv_sem,
):
    span, beams, chans = x_vmem.shape
    chips = send.shape[0]
    trials = offsets_vmem.shape[1]
    chunks = span // CHUNK_TIMES
    me = lax.axis_index("beam")
    core = lax.axis_index("sub")
    mesh_id = pl.DeviceIdType.MESH

    def load_chunk(index):
        part = pl.ds(index * CHUNK_TIMES, CHUNK_TIMES)
        return pltpu.make_async_copy(x_hbm.at[part], x_vmem.at[part], x_sem.at[index])

    first = pl.multiple_of((me * 2 + core) * chans, chans)
    delay_copy = pltpu.make_async_copy(
        delays_hbm.at[:, pl.ds(first, chans)], delays_vmem, small_sem.at[0]
    )
    half = pl.ds(pl.multiple_of(core * trials, trials), trials)
    offset_copy = pltpu.make_async_copy(offsets_hbm.at[:, half], offsets_vmem, small_sem.at[1])
    coarse_copy = pltpu.make_async_copy(coarse_hbm.at[:, half], coarse_vmem, small_sem.at[2])
    delay_copy.start()
    for index in range(chunks):
        load_chunk(index).start()
    offset_copy.start()
    coarse_copy.start()

    barrier = pltpu.get_barrier_semaphore()
    for step in range(1, chips):
        peer = lax.rem(me + step, chips)
        pl.semaphore_signal(barrier, inc=1, device_id={"beam": peer, "sub": core}, device_id_type=mesh_id)
    pl.semaphore_signal(barrier, inc=1, device_id={"beam": me, "sub": 1 - core}, device_id_type=mesh_id)

    delay_copy.wait()
    delays = delays_vmem[...]
    hits = [(delays == lag).astype(jnp.float32) for lag in range(BAND_LAGS)]
    table[...] = jnp.concatenate(hits, axis=0).T.astype(jnp.bfloat16)
    spread[span * beams :, :] = jnp.zeros((spread.shape[0] - span * beams, spread.shape[1]), jnp.float32)

    def multiply(index, carry):
        load_chunk(index).wait()
        rows = CHUNK_TIMES * beams
        block = x_vmem[pl.ds(index * CHUNK_TIMES, CHUNK_TIMES)].reshape(rows, chans)
        spread[pl.ds(pl.multiple_of(index * rows, rows), rows), :] = jnp.dot(
            block, table[...], preferred_element_type=jnp.float32
        )
        return carry

    lax.fori_loop(0, chunks, multiply, 0)

    def lagged(beam, start, count):
        lane_lag = lax.broadcasted_iota(jnp.int32, (count, BAND_LAGS * COARSE), 1) // COARSE
        total = spread[pl.ds(beam + beams * start, count, stride=beams), :]
        for lag in range(1, BAND_LAGS):
            later = spread[pl.ds(beam + beams * (start + lag), count, stride=beams), :]
            total = jnp.where(lane_lag == lag, later, total)
        return total

    def folded(rows):
        turned = rows.T
        total = turned[0:COARSE]
        for lag in range(1, BAND_LAGS):
            total = total + turned[lag * COARSE : (lag + 1) * COARSE]
        return total.astype(jnp.bfloat16)

    def beam_pair(chip):
        low = chip * 2
        blocks = []
        for beam in (low, low + 1):
            for start in (0, SAMPLE_LANES):
                blocks.append(folded(lagged(beam, start, SAMPLE_LANES)))
        ends = [lagged(beam, 2 * SAMPLE_LANES, 8) for beam in (low, low + 1)]
        ends.append(jnp.zeros((SAMPLE_LANES - 16, BAND_LAGS * COARSE), jnp.float32))
        blocks.append(folded(jnp.concatenate(ends, axis=0)))
        return blocks

    def send_copy(step):
        peer = lax.rem(me + step, chips)
        return pltpu.make_async_remote_copy(
            src_ref=send.at[peer],
            dst_ref=recv.at[me * 2 + core],
            send_sem=send_sem.at[step],
            recv_sem=recv_sem.at[me],
            device_id={"beam": peer, "sub": core},
            device_id_type=mesh_id,
        )

    def arrival(source):
        return pltpu.make_async_remote_copy(
            src_ref=send.at[source],
            dst_ref=recv.at[source * 2 + core],
            send_sem=send_sem.at[0],
            recv_sem=recv_sem.at[source],
            device_id={"beam": source, "sub": core},
            device_id_type=mesh_id,
        )

    def pass_copy(source, side):
        slot = recv.at[source * 2 + side]
        return pltpu.make_async_remote_copy(
            src_ref=slot,
            dst_ref=slot,
            send_sem=pass_send_sem.at[source],
            recv_sem=pass_recv_sem.at[source],
            device_id={"beam": me, "sub": 1 - core},
            device_id_type=mesh_id,
        )

    pl.semaphore_wait(barrier, chips)

    def send_pair(step, carry):
        peer = lax.rem(me + step, chips)
        for index, block in enumerate(beam_pair(peer)):
            send[peer, index] = block
        send_copy(step).start()
        return carry

    lax.fori_loop(1, chips, send_pair, 0)
    for index, block in enumerate(beam_pair(me)):
        recv[me * 2 + core, index] = block
    pass_copy(me, core).start()

    offset_copy.wait()
    coarse_copy.wait()
    coarse_ids = lax.broadcasted_iota(jnp.int32, (COARSE, trials), 0)
    coarse_hit = coarse_ids == coarse_vmem[...]
    offsets = offsets_vmem[...]
    keys = [
        jnp.where(coarse_hit, offsets[sub : sub + 1], -1).astype(jnp.float32)
        for sub in range(SUBBANDS)
    ]
    key_out[...] = jnp.concatenate(keys, axis=0).T.astype(jnp.bfloat16)

    for step in range(1, chips):
        source = lax.rem(me + chips - step, chips)
        arrival(source).wait_recv()
        pass_copy(source, core).start()
    for step in range(chips):
        source = lax.rem(me + chips - step, chips)
        pass_copy(source, 1 - core).wait_recv()
    for step in range(1, chips):
        send_copy(step).wait_send()
    for step in range(chips):
        source = lax.rem(me + chips - step, chips)
        pass_copy(source, core).wait_send()
    planes_out[...] = recv[...]


def trials_kernel(planes, key, out, shifted):
    rows = SUBBANDS * COARSE
    trials = key.shape[0]
    samples = 2 * SAMPLE_LANES
    keys = key[...]
    one, zero = jnp.bfloat16(1), jnp.bfloat16(0)
    table = jnp.concatenate(
        [jnp.where(keys == jnp.bfloat16(lag), one, zero) for lag in range(SUB_LAGS)], axis=1
    )
    for beam in range(2):
        parts = [planes[:, 2 * beam + index].reshape(rows, SAMPLE_LANES) for index in range(2)]
        end = planes[:, 4].reshape(rows, SAMPLE_LANES)
        whole = jnp.concatenate(parts + [end], axis=1).astype(jnp.float32)
        if beam:
            turned = pltpu.roll(whole[:, samples:], SAMPLE_LANES - 8 * beam, 1)
            whole = jnp.concatenate([whole[:, :samples], turned], axis=1)
        for lag in range(SUB_LAGS):
            moved = whole if lag == 0 else pltpu.roll(whole, whole.shape[1] - lag, 1)
            shifted[beam, lag * rows : (lag + 1) * rows, :] = moved[:, :samples].astype(jnp.bfloat16)
        out[:, beam, :] = jnp.dot(table, shifted[beam], preferred_element_type=jnp.float32)


def on_device_fused(intensities, sweep_delays, band_offsets, coarse_trial):
    beams, chans, span = intensities.shape
    chips = lax.axis_size("beam")
    trials = band_offsets.shape[1] // 2
    any_space = pl.BlockSpec(memory_space=pl.ANY)
    vmem = pl.BlockSpec(memory_space=pltpu.VMEM)
    cols = BAND_LAGS * COARSE
    rows = SUBBANDS * COARSE
    planes, key = pl.pallas_call(
        planes_kernel,
        out_shape=(
            jax.ShapeDtypeStruct((SUBBANDS, 5, COARSE, SAMPLE_LANES), jnp.bfloat16),
            jax.ShapeDtypeStruct((trials, rows), jnp.bfloat16),
        ),
        in_specs=[any_space] * 4,
        out_specs=(vmem, vmem),
        scratch_shapes=[
            pltpu.VMEM((span, beams, chans), jnp.bfloat16),
            pltpu.VMEM((COARSE, chans), jnp.int32),
            pltpu.VMEM((SUBBANDS, trials), jnp.int32),
            pltpu.VMEM((1, trials), jnp.int32),
            pltpu.VMEM((chans, cols), jnp.bfloat16),
            pltpu.VMEM(((span + 2) * beams, cols), jnp.float32),
            pltpu.VMEM((chips, 5, COARSE, SAMPLE_LANES), jnp.bfloat16),
            pltpu.VMEM((SUBBANDS, 5, COARSE, SAMPLE_LANES), jnp.bfloat16),
            pltpu.SemaphoreType.DMA((span // CHUNK_TIMES,)),
            pltpu.SemaphoreType.DMA((3,)),
            pltpu.SemaphoreType.DMA((chips,)),
            pltpu.SemaphoreType.DMA((chips,)),
            pltpu.SemaphoreType.DMA((chips,)),
            pltpu.SemaphoreType.DMA((chips,)),
        ],
        compiler_params=pltpu.CompilerParams(
            collective_id=0, has_side_effects=True, vmem_limit_bytes=40 * 2**20
        ),
        cost_estimate=pl.CostEstimate(
            flops=2 * span * beams * chans * cols,
            bytes_accessed=2 * span * beams * chans,
            transcendentals=0,
        ),
    )(
        jnp.transpose(intensities, (2, 0, 1)),
        sweep_delays.T,
        band_offsets,
        coarse_trial[None, :],
    )
    return pl.pallas_call(
        trials_kernel,
        out_shape=jax.ShapeDtypeStruct((trials, 2, 2 * SAMPLE_LANES), jnp.float32),
        in_specs=[vmem, vmem],
        out_specs=vmem,
        scratch_shapes=[pltpu.VMEM((2, SUB_LAGS * rows, 2 * SAMPLE_LANES), jnp.bfloat16)],
        compiler_params=pltpu.CompilerParams(vmem_limit_bytes=32 * 2**20),
        cost_estimate=pl.CostEstimate(
            flops=4 * trials * SUB_LAGS * rows * 2 * SAMPLE_LANES,
            bytes_accessed=16 * trials * SAMPLE_LANES,
            transcendentals=0,
        ),
    )(planes, key)


def program(intensities, sweep_delays, band_offsets, coarse_trial):
    beams, chans, span = intensities.shape
    chips, cores = lax.axis_size("beam"), lax.axis_size("sub")
    one_band = (
        chans == CHANNELS // SUBBANDS
        and cores == 2
        and chips * cores == SUBBANDS
        and beams == 2 * chips
        and beams == 16
        and span == 2 * SAMPLE_LANES + BAND_LAGS + SUB_LAGS - 2
        and span % CHUNK_TIMES == 0
    )
    chosen = on_device_fused if one_band else on_device
    return chosen(intensities, sweep_delays, band_offsets, coarse_trial)


def solution(mesh):
    in_specs = (P("groups", ("beam", "sub"), None), P(), P(), P())
    out_specs = P("sub", ("groups", "beam"), None)
    return jax.shard_map(
        program, mesh=mesh, in_specs=in_specs, out_specs=out_specs, check_vma=False
    )
```

```python
import jax
import jax.numpy as jnp
from jax import lax
from jax.experimental import pallas as pl
from jax.experimental.pallas import tpu as pltpu
from jax.sharding import PartitionSpec as P

CHANNELS = 16384
SUBBANDS = 16
COARSE = 16
BAND_LAGS = 8
SUB_LAGS = 8


def section_one(intens, delays, bands, span_out, groups):
    count_beams, chans, span = intens.shape
    block = min(chans, 1024)
    cols = groups * COARSE
    members = jnp.arange(groups, dtype=jnp.int32)
    lag_ids = jnp.arange(BAND_LAGS, dtype=jnp.int32)

    def add_block(index, total):
        member = bands[:, None] == members[None, :]
        lag_hit = delays[:, None, :] == lag_ids[None, :, None]
        table = (
            (member[:, None, :, None] & lag_hit[:, :, None, :])
            .reshape(block, BAND_LAGS * cols)
            .astype(jnp.bfloat16)
        )
        return total + jnp.einsum("bct,cn->btn", intens, table, preferred_element_type=jnp.float32)

    empty = jnp.zeros((count_beams, span, BAND_LAGS * cols), jnp.float32)
    spread = lax.fori_loop(0, chans // block, add_block, empty)
    result = spread[:, 0:span_out, 0:cols]
    for lag in range(1, BAND_LAGS):
        result = result + spread[:, lag : lag + span_out, lag * cols : (lag + 1) * cols]
    return result


def section_two(planes, offsets, coarse_map, count):
    halves_here, beams_here, span_out, cols = planes.shape
    samples = span_out - SUB_LAGS + 1
    coarse_hit = coarse_map[None, :] == jnp.arange(COARSE, dtype=jnp.int32)[:, None]
    total = jnp.zeros((count, beams_here, samples), jnp.float32)
    for lag in range(SUB_LAGS):
        table = (
            ((offsets == lag)[:, None, :] & coarse_hit[None, :, :])
            .reshape(cols, count)
            .astype(jnp.bfloat16)
        )
        total = total + jnp.einsum(
            "hbtn,nm->mbt",
            planes[:, :, lag : lag + samples, :],
            table,
            preferred_element_type=jnp.float32,
        )
    return total


def on_device(intensities, sweep_delays, band_offsets, coarse_trial):
    beams_all, chans_local, span = intensities.shape
    beam_count = lax.axis_size("beam")
    sub_count = lax.axis_size("sub")
    per_device = beams_all // beam_count
    out_len = span - BAND_LAGS + 1
    trials_local = band_offsets.shape[1] // sub_count
    sub_width = CHANNELS // SUBBANDS
    sub_here = lax.axis_index("sub")
    held = max(1, chans_local // sub_width)
    first = (lax.axis_index("beam") * sub_count + sub_here) * chans_local
    delay_view = lax.dynamic_slice_in_dim(sweep_delays, first, chans_local, 0)
    band_view = (first + jnp.arange(chans_local, dtype=jnp.int32)) // sub_width - first // sub_width
    local_terms = section_one(intensities, delay_view, band_view, out_len, held)
    grouped = local_terms.reshape(beam_count, per_device, out_len, held * COARSE)
    arrived = lax.all_to_all(grouped, "beam", split_axis=0, concat_axis=0, tiled=True)
    arrived = arrived.reshape(beam_count, per_device, out_len, held, COARSE)
    source_first = (
        (jnp.arange(beam_count, dtype=jnp.int32) * sub_count + sub_here) * chans_local // sub_width
    )
    target = source_first[:, None] + jnp.arange(held, dtype=jnp.int32)[None, :]
    placing = (target[:, :, None] == jnp.arange(SUBBANDS, dtype=jnp.int32)[None, None, :]).astype(
        jnp.float32
    )
    planes = jnp.einsum(
        "ibtpc,ips->btsc", arrived, placing, precision=lax.Precision.HIGHEST
    ).reshape(per_device, out_len, SUBBANDS * COARSE)
    rounded = planes.astype(jnp.bfloat16)
    return lax.psum_scatter(
        section_two(rounded[None], band_offsets, coarse_trial, lax.axis_size("sub") * trials_local),
        "sub",
        scatter_dimension=0,
        tiled=True,
    )


SAMPLE_LANES = 128
CHUNK_TIMES = 30
CHOOSE_TIMES = 10


def planes_kernel(
    x_hbm,
    delays_hbm,
    offsets_hbm,
    coarse_hbm,
    planes_out,
    key_out,
    x_vmem,
    delays_vmem,
    offsets_vmem,
    coarse_vmem,
    table,
    spread,
    chosen,
    send_low,
    send_high,
    recv_low,
    recv_high,
    x_sem,
    small_sem,
    send_sem,
    recv_sem,
    pass_send_sem,
    pass_recv_sem,
):
    span, beams, chans = x_vmem.shape
    chips = send_low.shape[0]
    trials = offsets_vmem.shape[1]
    chunks = span // CHUNK_TIMES
    times = chosen.shape[0] // beams
    cols = BAND_LAGS * COARSE
    me = lax.axis_index("beam")
    core = lax.axis_index("sub")
    mesh_id = pl.DeviceIdType.MESH
    sends, recvs = (send_low, send_high), (recv_low, recv_high)

    def load_chunk(index):
        part = pl.ds(index * CHUNK_TIMES, CHUNK_TIMES)
        return pltpu.make_async_copy(x_hbm.at[part], x_vmem.at[part], x_sem.at[index])

    first = pl.multiple_of((me * 2 + core) * chans, chans)
    delay_copy = pltpu.make_async_copy(
        delays_hbm.at[:, pl.ds(first, chans)], delays_vmem, small_sem.at[0]
    )
    half = pl.ds(pl.multiple_of(core * trials, trials), trials)
    offset_copy = pltpu.make_async_copy(offsets_hbm.at[:, half], offsets_vmem, small_sem.at[1])
    coarse_copy = pltpu.make_async_copy(coarse_hbm.at[:, half], coarse_vmem, small_sem.at[2])
    delay_copy.start()
    for index in range(chunks):
        load_chunk(index).start()
    offset_copy.start()
    coarse_copy.start()

    barrier = pltpu.get_barrier_semaphore()
    for step in range(1, chips):
        peer = lax.rem(me + step, chips)
        pl.semaphore_signal(barrier, inc=1, device_id={"beam": peer, "sub": core}, device_id_type=mesh_id)
    pl.semaphore_signal(barrier, inc=1, device_id={"beam": me, "sub": 1 - core}, device_id_type=mesh_id)

    delay_copy.wait()
    delays = delays_vmem[...]
    hits = [(delays == lag).astype(jnp.float32) for lag in range(BAND_LAGS)]
    table[...] = jnp.concatenate(hits, axis=0).T.astype(jnp.bfloat16)
    spread[span * beams :, :] = jnp.zeros((spread.shape[0] - span * beams, cols), jnp.float32)
    rows = CHUNK_TIMES * beams

    def multiply(index):
        block = x_vmem[index * CHUNK_TIMES : (index + 1) * CHUNK_TIMES].reshape(rows, chans)
        spread[index * rows : (index + 1) * rows, :] = jnp.dot(
            block, table[...], preferred_element_type=jnp.float32
        )

    def choose(start, stop):
        for low in range(start, stop, CHOOSE_TIMES):
            count = min(CHOOSE_TIMES, stop - low)
            value = spread[low * beams : (low + count + BAND_LAGS - 1) * beams, :]
            for bit in (1, 2, 4):
                size = value.shape[0] - bit * beams
                lane_lag = lax.broadcasted_iota(jnp.int32, (size, cols), 1) // COARSE
                value = jnp.where(lane_lag & bit != 0, value[bit * beams :], value[:size])
            chosen[low * beams : (low + count) * beams, :] = value

    def folded(part):
        turned = part.T
        total = turned[0:COARSE]
        for lag in range(1, BAND_LAGS):
            total = total + turned[lag * COARSE : (lag + 1) * COARSE]
        return total.astype(jnp.bfloat16)

    def half_block(beam, start):
        return folded(chosen[pl.ds(beam + beams * start, SAMPLE_LANES, stride=beams), :])

    def send_copy(part, step):
        peer = lax.rem(me + step, chips)
        return pltpu.make_async_remote_copy(
            src_ref=sends[part].at[peer],
            dst_ref=recvs[part].at[me * 2 + core],
            send_sem=send_sem.at[part, step],
            recv_sem=recv_sem.at[part, me],
            device_id={"beam": peer, "sub": core},
            device_id_type=mesh_id,
        )

    def arrival(part, source):
        return pltpu.make_async_remote_copy(
            src_ref=sends[part].at[source],
            dst_ref=recvs[part].at[source * 2 + core],
            send_sem=send_sem.at[part, 0],
            recv_sem=recv_sem.at[part, source],
            device_id={"beam": source, "sub": core},
            device_id_type=mesh_id,
        )

    def pass_copy(part, source, side):
        slot = recvs[part].at[source * 2 + side]
        return pltpu.make_async_remote_copy(
            src_ref=slot,
            dst_ref=slot,
            send_sem=pass_send_sem.at[part, source],
            recv_sem=pass_recv_sem.at[part, source],
            device_id={"beam": me, "sub": 1 - core},
            device_id_type=mesh_id,
        )

    def send_part(part, ends):
        start = part * SAMPLE_LANES

        def send_pair(step, carry):
            peer = lax.rem(me + step, chips)
            for beam in range(2):
                sends[part][peer, beam] = half_block(peer * 2 + beam, start)
            if ends is not None:
                sends[part][peer, 2] = ends
            send_copy(part, step).start()
            return carry

        lax.fori_loop(1, chips, send_pair, 0)
        for beam in range(2):
            recvs[part][me * 2 + core, beam] = half_block(me * 2 + beam, start)
        if ends is not None:
            recvs[part][me * 2 + core, 2] = ends
        pass_copy(part, me, core).start()

    def pass_on(part):
        for step in range(1, chips):
            source = lax.rem(me + chips - step, chips)
            arrival(part, source).wait_recv()
            pass_copy(part, source, core).start()

    done = 0
    sent = False
    for index in range(chunks + 1):
        if index < chunks:
            load_chunk(index).wait()
            multiply(index)
        if index:
            ready = times if index == chunks else index * CHUNK_TIMES - BAND_LAGS + 1
            choose(done, ready)
            done = ready
        if not sent and done >= SAMPLE_LANES:
            sent = True
            pl.semaphore_wait(barrier, chips)
            send_part(0, None)
    ends = [
        chosen[pl.ds(beam + 2 * SAMPLE_LANES * beams, 8, stride=beams), :] for beam in range(beams)
    ]
    send_part(1, folded(jnp.concatenate(ends, axis=0)))

    offset_copy.wait()
    coarse_copy.wait()
    coarse_ids = lax.broadcasted_iota(jnp.int32, (COARSE, trials), 0)
    coarse_hit = coarse_ids == coarse_vmem[...]
    offsets = offsets_vmem[...]
    keys = [
        jnp.where(coarse_hit, offsets[sub : sub + 1], -1).astype(jnp.float32)
        for sub in range(SUBBANDS)
    ]
    key_out[...] = jnp.concatenate(keys, axis=0).T.astype(jnp.bfloat16)

    pass_on(0)
    pass_on(1)
    for part in range(2):
        for step in range(chips):
            source = lax.rem(me + chips - step, chips)
            pass_copy(part, source, 1 - core).wait_recv()
    for index, (part, place) in enumerate(((0, 0), (1, 0), (0, 1), (1, 1), (1, 2))):
        planes_out[:, index] = recvs[part][:, place]
    for part in range(2):
        for step in range(1, chips):
            send_copy(part, step).wait_send()
        for step in range(chips):
            source = lax.rem(me + chips - step, chips)
            pass_copy(part, source, core).wait_send()


def trials_kernel(planes, key, out, shifted):
    rows = SUBBANDS * COARSE
    trials = key.shape[0]
    samples = 2 * SAMPLE_LANES
    me = lax.axis_index("beam")
    keys = key[...]
    one, zero = jnp.bfloat16(1), jnp.bfloat16(0)
    table = jnp.concatenate(
        [jnp.where(keys == jnp.bfloat16(lag), one, zero) for lag in range(SUB_LAGS)], axis=1
    )
    for beam in range(2):
        parts = [planes[:, 2 * beam + index].reshape(rows, SAMPLE_LANES) for index in range(2)]
        end = planes[:, 4].reshape(rows, SAMPLE_LANES)
        whole = jnp.concatenate(parts + [end], axis=1).astype(jnp.float32)
        back = lax.rem(SAMPLE_LANES - 8 * (2 * me + beam), SAMPLE_LANES)
        turned = pltpu.roll(whole[:, samples:], back, 1)
        whole = jnp.concatenate([whole[:, :samples], turned], axis=1)
        for lag in range(SUB_LAGS):
            moved = whole if lag == 0 else pltpu.roll(whole, whole.shape[1] - lag, 1)
            shifted[beam, lag * rows : (lag + 1) * rows, :] = moved[:, :samples].astype(jnp.bfloat16)
        out[:, beam, :] = jnp.dot(table, shifted[beam], preferred_element_type=jnp.float32)


def on_device_fused(intensities, sweep_delays, band_offsets, coarse_trial):
    beams, chans, span = intensities.shape
    chips = lax.axis_size("beam")
    trials = band_offsets.shape[1] // 2
    any_space = pl.BlockSpec(memory_space=pl.ANY)
    vmem = pl.BlockSpec(memory_space=pltpu.VMEM)
    cols = BAND_LAGS * COARSE
    rows = SUBBANDS * COARSE
    planes, key = pl.pallas_call(
        planes_kernel,
        out_shape=(
            jax.ShapeDtypeStruct((SUBBANDS, 5, COARSE, SAMPLE_LANES), jnp.bfloat16),
            jax.ShapeDtypeStruct((trials, rows), jnp.bfloat16),
        ),
        in_specs=[any_space] * 4,
        out_specs=(vmem, vmem),
        scratch_shapes=[
            pltpu.VMEM((span, beams, chans), jnp.bfloat16),
            pltpu.VMEM((COARSE, chans), jnp.int32),
            pltpu.VMEM((SUBBANDS, trials), jnp.int32),
            pltpu.VMEM((1, trials), jnp.int32),
            pltpu.VMEM((chans, cols), jnp.bfloat16),
            pltpu.VMEM(((span + 2) * beams, cols), jnp.float32),
            pltpu.VMEM(((2 * SAMPLE_LANES + 8) * beams, cols), jnp.float32),
            pltpu.VMEM((chips, 2, COARSE, SAMPLE_LANES), jnp.bfloat16),
            pltpu.VMEM((chips, 3, COARSE, SAMPLE_LANES), jnp.bfloat16),
            pltpu.VMEM((SUBBANDS, 2, COARSE, SAMPLE_LANES), jnp.bfloat16),
            pltpu.VMEM((SUBBANDS, 3, COARSE, SAMPLE_LANES), jnp.bfloat16),
            pltpu.SemaphoreType.DMA((span // CHUNK_TIMES,)),
            pltpu.SemaphoreType.DMA((3,)),
            pltpu.SemaphoreType.DMA((2, chips)),
            pltpu.SemaphoreType.DMA((2, chips)),
            pltpu.SemaphoreType.DMA((2, chips)),
            pltpu.SemaphoreType.DMA((2, chips)),
        ],
        compiler_params=pltpu.CompilerParams(
            collective_id=0, has_side_effects=True, vmem_limit_bytes=62 * 2**20
        ),
        cost_estimate=pl.CostEstimate(
            flops=2 * span * beams * chans * cols,
            bytes_accessed=2 * span * beams * chans,
            transcendentals=0,
        ),
    )(
        jnp.transpose(intensities, (2, 0, 1)),
        sweep_delays.T,
        band_offsets,
        coarse_trial[None, :],
    )
    return pl.pallas_call(
        trials_kernel,
        out_shape=jax.ShapeDtypeStruct((trials, 2, 2 * SAMPLE_LANES), jnp.float32),
        in_specs=[vmem, vmem],
        out_specs=vmem,
        scratch_shapes=[pltpu.VMEM((2, SUB_LAGS * rows, 2 * SAMPLE_LANES), jnp.bfloat16)],
        compiler_params=pltpu.CompilerParams(vmem_limit_bytes=62 * 2**20),
        cost_estimate=pl.CostEstimate(
            flops=4 * trials * SUB_LAGS * rows * 2 * SAMPLE_LANES,
            bytes_accessed=16 * trials * SAMPLE_LANES,
            transcendentals=0,
        ),
    )(planes, key)


def program(intensities, sweep_delays, band_offsets, coarse_trial):
    beams, chans, span = intensities.shape
    chips, cores = lax.axis_size("beam"), lax.axis_size("sub")
    one_band = (
        chans == CHANNELS // SUBBANDS
        and cores == 2
        and chips * cores == SUBBANDS
        and beams == 2 * chips
        and beams == 16
        and span == 2 * SAMPLE_LANES + BAND_LAGS + SUB_LAGS - 2
        and span % CHUNK_TIMES == 0
    )
    chosen = on_device_fused if one_band else on_device
    return chosen(intensities, sweep_delays, band_offsets, coarse_trial)


def solution(mesh):
    in_specs = (P("groups", ("beam", "sub"), None), P(), P(), P())
    out_specs = P("sub", ("groups", "beam"), None)
    return jax.shard_map(
        program, mesh=mesh, in_specs=in_specs, out_specs=out_specs, check_vma=False
    )
```

```python
import jax
import jax.numpy as jnp
from jax import lax
from jax.experimental import pallas as pl
from jax.experimental.pallas import tpu as pltpu
from jax.sharding import PartitionSpec as P

CHANNELS = 16384
SUBBANDS = 16
COARSE = 16
BAND_LAGS = 8
SUB_LAGS = 8


def section_one(intens, delays, bands, span_out, groups):
    count_beams, chans, span = intens.shape
    block = min(chans, 1024)
    cols = groups * COARSE
    members = jnp.arange(groups, dtype=jnp.int32)
    lag_ids = jnp.arange(BAND_LAGS, dtype=jnp.int32)

    def add_block(index, total):
        member = bands[:, None] == members[None, :]
        lag_hit = delays[:, None, :] == lag_ids[None, :, None]
        table = (
            (member[:, None, :, None] & lag_hit[:, :, None, :])
            .reshape(block, BAND_LAGS * cols)
            .astype(jnp.bfloat16)
        )
        return total + jnp.einsum("bct,cn->btn", intens, table, preferred_element_type=jnp.float32)

    empty = jnp.zeros((count_beams, span, BAND_LAGS * cols), jnp.float32)
    spread = lax.fori_loop(0, chans // block, add_block, empty)
    result = spread[:, 0:span_out, 0:cols]
    for lag in range(1, BAND_LAGS):
        result = result + spread[:, lag : lag + span_out, lag * cols : (lag + 1) * cols]
    return result


def section_two(planes, offsets, coarse_map, count):
    halves_here, beams_here, span_out, cols = planes.shape
    samples = span_out - SUB_LAGS + 1
    coarse_hit = coarse_map[None, :] == jnp.arange(COARSE, dtype=jnp.int32)[:, None]
    total = jnp.zeros((count, beams_here, samples), jnp.float32)
    for lag in range(SUB_LAGS):
        table = (
            ((offsets == lag)[:, None, :] & coarse_hit[None, :, :])
            .reshape(cols, count)
            .astype(jnp.bfloat16)
        )
        total = total + jnp.einsum(
            "hbtn,nm->mbt",
            planes[:, :, lag : lag + samples, :],
            table,
            preferred_element_type=jnp.float32,
        )
    return total


def on_device(intensities, sweep_delays, band_offsets, coarse_trial):
    beams_all, chans_local, span = intensities.shape
    beam_count = lax.axis_size("beam")
    sub_count = lax.axis_size("sub")
    per_device = beams_all // beam_count
    out_len = span - BAND_LAGS + 1
    trials_local = band_offsets.shape[1] // sub_count
    sub_width = CHANNELS // SUBBANDS
    sub_here = lax.axis_index("sub")
    held = max(1, chans_local // sub_width)
    first = (lax.axis_index("beam") * sub_count + sub_here) * chans_local
    delay_view = lax.dynamic_slice_in_dim(sweep_delays, first, chans_local, 0)
    band_view = (first + jnp.arange(chans_local, dtype=jnp.int32)) // sub_width - first // sub_width
    local_terms = section_one(intensities, delay_view, band_view, out_len, held)
    grouped = local_terms.reshape(beam_count, per_device, out_len, held * COARSE)
    arrived = lax.all_to_all(grouped, "beam", split_axis=0, concat_axis=0, tiled=True)
    arrived = arrived.reshape(beam_count, per_device, out_len, held, COARSE)
    source_first = (
        (jnp.arange(beam_count, dtype=jnp.int32) * sub_count + sub_here) * chans_local // sub_width
    )
    target = source_first[:, None] + jnp.arange(held, dtype=jnp.int32)[None, :]
    placing = (target[:, :, None] == jnp.arange(SUBBANDS, dtype=jnp.int32)[None, None, :]).astype(
        jnp.float32
    )
    planes = jnp.einsum(
        "ibtpc,ips->btsc", arrived, placing, precision=lax.Precision.HIGHEST
    ).reshape(per_device, out_len, SUBBANDS * COARSE)
    rounded = planes.astype(jnp.bfloat16)
    return lax.psum_scatter(
        section_two(rounded[None], band_offsets, coarse_trial, lax.axis_size("sub") * trials_local),
        "sub",
        scatter_dimension=0,
        tiled=True,
    )


SAMPLE_LANES = 128
CHUNK_TIMES = 54
CHOOSE_TIMES = 10


def planes_kernel(
    x_hbm,
    delays_hbm,
    offsets_hbm,
    coarse_hbm,
    planes_out,
    key_out,
    x_vmem,
    delays_vmem,
    offsets_vmem,
    coarse_vmem,
    table,
    spread,
    chosen,
    send_low,
    send_high,
    recv_low,
    recv_high,
    x_sem,
    small_sem,
    send_sem,
    recv_sem,
    pass_send_sem,
    pass_recv_sem,
):
    span, beams, chans = x_vmem.shape
    chips = send_low.shape[0]
    trials = offsets_vmem.shape[1]
    chunks = span // CHUNK_TIMES
    times = chosen.shape[0] // beams
    cols = BAND_LAGS * COARSE
    me = lax.axis_index("beam")
    core = lax.axis_index("sub")
    mesh_id = pl.DeviceIdType.MESH
    sends, recvs = (send_low, send_high), (recv_low, recv_high)

    def load_chunk(index):
        part = pl.ds(index * CHUNK_TIMES, CHUNK_TIMES)
        return pltpu.make_async_copy(x_hbm.at[part], x_vmem.at[part], x_sem.at[index])

    first = pl.multiple_of((me * 2 + core) * chans, chans)
    delay_copy = pltpu.make_async_copy(
        delays_hbm.at[:, pl.ds(first, chans)], delays_vmem, small_sem.at[0]
    )
    half = pl.ds(pl.multiple_of(core * trials, trials), trials)
    offset_copy = pltpu.make_async_copy(offsets_hbm.at[:, half], offsets_vmem, small_sem.at[1])
    coarse_copy = pltpu.make_async_copy(coarse_hbm.at[:, half], coarse_vmem, small_sem.at[2])
    delay_copy.start()
    for index in range(chunks):
        load_chunk(index).start()
    offset_copy.start()
    coarse_copy.start()

    barrier = pltpu.get_barrier_semaphore()
    for step in range(1, chips):
        peer = lax.rem(me + step, chips)
        pl.semaphore_signal(barrier, inc=1, device_id={"beam": peer, "sub": core}, device_id_type=mesh_id)
    pl.semaphore_signal(barrier, inc=1, device_id={"beam": me, "sub": 1 - core}, device_id_type=mesh_id)

    delay_copy.wait()
    delays = delays_vmem[...]
    hits = [(delays == lag).astype(jnp.float32) for lag in range(BAND_LAGS)]
    table[...] = jnp.concatenate(hits, axis=0).T.astype(jnp.bfloat16)
    spread[span * beams :, :] = jnp.zeros((spread.shape[0] - span * beams, cols), jnp.float32)
    rows = CHUNK_TIMES * beams

    def multiply(index):
        block = x_vmem[index * CHUNK_TIMES : (index + 1) * CHUNK_TIMES].reshape(rows, chans)
        spread[index * rows : (index + 1) * rows, :] = jnp.dot(
            block, table[...], preferred_element_type=jnp.float32
        )

    def choose(start, stop):
        for low in range(start, stop, CHOOSE_TIMES):
            count = min(CHOOSE_TIMES, stop - low)
            value = spread[low * beams : (low + count + BAND_LAGS - 1) * beams, :]
            for bit in (1, 2, 4):
                size = value.shape[0] - bit * beams
                lane_lag = lax.broadcasted_iota(jnp.int32, (size, cols), 1) // COARSE
                value = jnp.where(lane_lag & bit != 0, value[bit * beams :], value[:size])
            chosen[low * beams : (low + count) * beams, :] = value

    def folded(part):
        turned = part.T
        total = turned[0:COARSE]
        for lag in range(1, BAND_LAGS):
            total = total + turned[lag * COARSE : (lag + 1) * COARSE]
        return total.astype(jnp.bfloat16)

    def half_block(beam, start):
        return folded(chosen[pl.ds(beam + beams * start, SAMPLE_LANES, stride=beams), :])

    def send_copy(part, step):
        peer = lax.rem(me + step, chips)
        return pltpu.make_async_remote_copy(
            src_ref=sends[part].at[peer],
            dst_ref=recvs[part].at[me * 2 + core],
            send_sem=send_sem.at[part, step],
            recv_sem=recv_sem.at[part, me],
            device_id={"beam": peer, "sub": core},
            device_id_type=mesh_id,
        )

    def arrival(part, source):
        return pltpu.make_async_remote_copy(
            src_ref=sends[part].at[source],
            dst_ref=recvs[part].at[source * 2 + core],
            send_sem=send_sem.at[part, 0],
            recv_sem=recv_sem.at[part, source],
            device_id={"beam": source, "sub": core},
            device_id_type=mesh_id,
        )

    def pass_copy(part, source, side):
        slot = recvs[part].at[source * 2 + side]
        return pltpu.make_async_remote_copy(
            src_ref=slot,
            dst_ref=slot,
            send_sem=pass_send_sem.at[part, source],
            recv_sem=pass_recv_sem.at[part, source],
            device_id={"beam": me, "sub": 1 - core},
            device_id_type=mesh_id,
        )

    def send_part(part, ends):
        start = part * SAMPLE_LANES

        def send_pair(step, carry):
            peer = lax.rem(me + step, chips)
            for beam in range(2):
                sends[part][peer, beam] = half_block(peer * 2 + beam, start)
            if ends is not None:
                sends[part][peer, 2] = ends
            send_copy(part, step).start()
            return carry

        lax.fori_loop(1, chips, send_pair, 0)
        for beam in range(2):
            recvs[part][me * 2 + core, beam] = half_block(me * 2 + beam, start)
        if ends is not None:
            recvs[part][me * 2 + core, 2] = ends
        pass_copy(part, me, core).start()

    def pass_on(part):
        for step in range(1, chips):
            source = lax.rem(me + chips - step, chips)
            arrival(part, source).wait_recv()
            pass_copy(part, source, core).start()

    done = 0
    sent = False
    for index in range(chunks + 1):
        if index < chunks:
            load_chunk(index).wait()
            multiply(index)
        if index:
            ready = times if index == chunks else index * CHUNK_TIMES - BAND_LAGS + 1
            choose(done, ready)
            done = ready
        if not sent and done >= SAMPLE_LANES:
            sent = True
            pl.semaphore_wait(barrier, chips)
            send_part(0, None)
    ends = [
        chosen[pl.ds(beam + 2 * SAMPLE_LANES * beams, 8, stride=beams), :] for beam in range(beams)
    ]
    send_part(1, folded(jnp.concatenate(ends, axis=0)))

    offset_copy.wait()
    coarse_copy.wait()
    coarse_ids = lax.broadcasted_iota(jnp.int32, (COARSE, trials), 0)
    coarse_hit = coarse_ids == coarse_vmem[...]
    offsets = offsets_vmem[...]
    keys = [
        jnp.where(coarse_hit, offsets[sub : sub + 1], -1).astype(jnp.float32)
        for sub in range(SUBBANDS)
    ]
    key_out[...] = jnp.concatenate(keys, axis=0).T.astype(jnp.bfloat16)

    pass_on(0)
    pass_on(1)
    for part in range(2):
        for step in range(chips):
            source = lax.rem(me + chips - step, chips)
            pass_copy(part, source, 1 - core).wait_recv()
    for index, (part, place) in enumerate(((0, 0), (1, 0), (0, 1), (1, 1), (1, 2))):
        planes_out[:, index] = recvs[part][:, place]
    for part in range(2):
        for step in range(1, chips):
            send_copy(part, step).wait_send()
        for step in range(chips):
            source = lax.rem(me + chips - step, chips)
            pass_copy(part, source, core).wait_send()


def trials_kernel(planes, key, out, shifted):
    rows = SUBBANDS * COARSE
    trials = key.shape[0]
    samples = 2 * SAMPLE_LANES
    me = lax.axis_index("beam")
    keys = key[...]
    one, zero = jnp.bfloat16(1), jnp.bfloat16(0)
    table = jnp.concatenate(
        [jnp.where(keys == jnp.bfloat16(lag), one, zero) for lag in range(SUB_LAGS)], axis=1
    )
    for beam in range(2):
        parts = [planes[:, 2 * beam + index].reshape(rows, SAMPLE_LANES) for index in range(2)]
        end = planes[:, 4].reshape(rows, SAMPLE_LANES)
        whole = jnp.concatenate(parts + [end], axis=1).astype(jnp.float32)
        back = lax.rem(SAMPLE_LANES - 8 * (2 * me + beam), SAMPLE_LANES)
        turned = pltpu.roll(whole[:, samples:], back, 1)
        whole = jnp.concatenate([whole[:, :samples], turned], axis=1)
        for lag in range(SUB_LAGS):
            moved = whole if lag == 0 else pltpu.roll(whole, whole.shape[1] - lag, 1)
            shifted[beam, lag * rows : (lag + 1) * rows, :] = moved[:, :samples].astype(jnp.bfloat16)
        out[:, beam, :] = jnp.dot(table, shifted[beam], preferred_element_type=jnp.float32)


def on_device_fused(intensities, sweep_delays, band_offsets, coarse_trial):
    beams, chans, span = intensities.shape
    chips = lax.axis_size("beam")
    trials = band_offsets.shape[1] // 2
    any_space = pl.BlockSpec(memory_space=pl.ANY)
    vmem = pl.BlockSpec(memory_space=pltpu.VMEM)
    cols = BAND_LAGS * COARSE
    rows = SUBBANDS * COARSE
    planes, key = pl.pallas_call(
        planes_kernel,
        out_shape=(
            jax.ShapeDtypeStruct((SUBBANDS, 5, COARSE, SAMPLE_LANES), jnp.bfloat16),
            jax.ShapeDtypeStruct((trials, rows), jnp.bfloat16),
        ),
        in_specs=[any_space] * 4,
        out_specs=(vmem, vmem),
        scratch_shapes=[
            pltpu.VMEM((span, beams, chans), jnp.bfloat16),
            pltpu.VMEM((COARSE, chans), jnp.int32),
            pltpu.VMEM((SUBBANDS, trials), jnp.int32),
            pltpu.VMEM((1, trials), jnp.int32),
            pltpu.VMEM((chans, cols), jnp.bfloat16),
            pltpu.VMEM(((span + 2) * beams, cols), jnp.float32),
            pltpu.VMEM(((2 * SAMPLE_LANES + 8) * beams, cols), jnp.float32),
            pltpu.VMEM((chips, 2, COARSE, SAMPLE_LANES), jnp.bfloat16),
            pltpu.VMEM((chips, 3, COARSE, SAMPLE_LANES), jnp.bfloat16),
            pltpu.VMEM((SUBBANDS, 2, COARSE, SAMPLE_LANES), jnp.bfloat16),
            pltpu.VMEM((SUBBANDS, 3, COARSE, SAMPLE_LANES), jnp.bfloat16),
            pltpu.SemaphoreType.DMA((span // CHUNK_TIMES,)),
            pltpu.SemaphoreType.DMA((3,)),
            pltpu.SemaphoreType.DMA((2, chips)),
            pltpu.SemaphoreType.DMA((2, chips)),
            pltpu.SemaphoreType.DMA((2, chips)),
            pltpu.SemaphoreType.DMA((2, chips)),
        ],
        compiler_params=pltpu.CompilerParams(
            collective_id=0, has_side_effects=True, vmem_limit_bytes=62 * 2**20
        ),
        cost_estimate=pl.CostEstimate(
            flops=2 * span * beams * chans * cols,
            bytes_accessed=2 * span * beams * chans,
            transcendentals=0,
        ),
    )(
        jnp.transpose(intensities, (2, 0, 1)),
        sweep_delays.T,
        band_offsets,
        coarse_trial[None, :],
    )
    return pl.pallas_call(
        trials_kernel,
        out_shape=jax.ShapeDtypeStruct((trials, 2, 2 * SAMPLE_LANES), jnp.float32),
        in_specs=[vmem, vmem],
        out_specs=vmem,
        scratch_shapes=[pltpu.VMEM((2, SUB_LAGS * rows, 2 * SAMPLE_LANES), jnp.bfloat16)],
        compiler_params=pltpu.CompilerParams(vmem_limit_bytes=62 * 2**20),
        cost_estimate=pl.CostEstimate(
            flops=4 * trials * SUB_LAGS * rows * 2 * SAMPLE_LANES,
            bytes_accessed=16 * trials * SAMPLE_LANES,
            transcendentals=0,
        ),
    )(planes, key)


def program(intensities, sweep_delays, band_offsets, coarse_trial):
    beams, chans, span = intensities.shape
    chips, cores = lax.axis_size("beam"), lax.axis_size("sub")
    one_band = (
        chans == CHANNELS // SUBBANDS
        and cores == 2
        and chips * cores == SUBBANDS
        and beams == 2 * chips
        and beams == 16
        and span == 2 * SAMPLE_LANES + BAND_LAGS + SUB_LAGS - 2
        and span % CHUNK_TIMES == 0
    )
    chosen = on_device_fused if one_band else on_device
    return chosen(intensities, sweep_delays, band_offsets, coarse_trial)


def solution(mesh):
    in_specs = (P("groups", ("beam", "sub"), None), P(), P(), P())
    out_specs = P("sub", ("groups", "beam"), None)
    return jax.shard_map(
        program, mesh=mesh, in_specs=in_specs, out_specs=out_specs, check_vma=False
    )
```
